32 devices in a mesh: ctx: 8 (over y, x, core), head: 4 (over z).
Axes of the slice: x: 2, y: 2, z: 4, core: 2. Of those that a mesh axis runs over, the one named last changes fastest.
Arguments:
- block_order: int32 [16], replicated, may hold values from 0 to 15, each once
- queries: bfloat16 [1792, 32, 576], P('ctx', 'head'), may hold values from -10 to 10
- keys: bfloat16 [1792, 576], P('ctx'), may hold values from -4 to 4
- dout: bfloat16 [1792, 32, 512], P('ctx', 'head'), may hold values from -6 to 6
Outputs:
- grad_queries: bfloat16 [1792, 32, 576], P('ctx', 'head')
- grad_keys: float32 [1792, 576], P('ctx')
The draws below stay inside these ranges and needn't reach their ends.
Inputs may be any that keep to these rules, and one draw needn't show every extreme that they name: block_order holds each of 0 to 15 once.
All inputs are finite; a program needn't handle non-finite values.
Results may differ from the reference program's by a relative error of at most 0.0048.
Values may be sent and summed in bfloat16 or wider, within the bound.
No kernel may reach another device: no remote copies, remote signals or barrier semaphores. Data moves between devices by JAX's collectives and lax.ppermute only.
A program may use at most 64 MiB of HBM per device.

```python
import jax
import jax.numpy as jnp
from jax import lax

LAT = 512
ROPE = 64
KDIM = 576
HEADS = 32
SEQ = 1792
BLOCKS = 16


def paired_arrays(key):
    first = jax.random.fold_in(key, 101)
    second = jax.random.fold_in(key, 202)
    third = jax.random.fold_in(key, 303)
    fourth = jax.random.fold_in(key, 404)
    latent = jax.random.truncated_normal(first, -4.0, 4.0, (SEQ, LAT), jnp.float32)
    rotary = jax.random.truncated_normal(second, -4.0, 4.0, (SEQ, ROPE), jnp.float32)
    query_latent = 0.5 * jax.random.truncated_normal(third, -4.0, 4.0, (SEQ, HEADS, LAT), jnp.float32)
    query_rotary = jax.random.truncated_normal(fourth, -4.0, 4.0, (SEQ, HEADS, ROPE), jnp.float32)
    key_array = jnp.concatenate([latent, rotary], axis=1)
    query_array = jnp.concatenate([query_latent, query_rotary], axis=2)
    return (key_array, query_array)


def draw_keys(key, part):
    key_array, query_array = paired_arrays(key)
    return key_array.astype(jnp.bfloat16)


def draw_queries(key, part):
    key_array, query_array = paired_arrays(key)
    return query_array.astype(jnp.bfloat16)


def levels(key, extent, split, smallest, high):
    def one(position, shards_of):
        heights = jax.random.uniform(jax.random.fold_in(jax.random.fold_in(key, 6), position), (shards_of,), jnp.float32, smallest / len(split), high / len(split))
        return jnp.repeat(jnp.exp(heights), extent[position] // shards_of).reshape((-1,) + (1,) * (len(extent) - position - 1))

    factor_of = one(*split[0])
    for cut in split[1:]:
        factor_of = factor_of * one(*cut)
    return factor_of


def noise(own_key, shape, spread, limit, pieces=(), kind=jnp.bfloat16):
    loudness = levels(own_key, shape, pieces, -0.22, 0.18) if pieces else 1.0
    drawn = jax.random.normal(own_key, shape, jnp.float32) * spread * loudness
    return jnp.minimum(jnp.maximum(drawn, -limit), limit).astype(kind)


def setup_inputs(seed: int = 0) -> dict:
    splits = jax.random.split(jax.random.key(seed), 5)
    block_order = jax.random.permutation(splits[0], BLOCKS).astype(jnp.int32)
    queries = draw_queries(jax.random.fold_in(splits[4], 71), 0)
    keys = draw_keys(jax.random.fold_in(splits[4], 71), 0)
    dout = noise(splits[3], (SEQ, HEADS, LAT), 1.0, 6.0, ((0, 8), (1, 4)))
    return {"block_order": block_order, "queries": queries, "keys": keys, "dout": dout}


softmax_scale = 0.1352
masked_value = -1e30


def reference(block_order, queries, keys, dout):
    block_rows = SEQ // BLOCKS
    offsets = jnp.arange(block_rows, dtype=jnp.int32)
    positions = (block_order[:, None].astype(jnp.int32) * block_rows + offsets[None, :]).reshape(SEQ)
    visible = positions[None, :] <= positions[:, None]
    latent_keys = keys[:, :LAT]

    def per_head(total, head_items):
        query, grad_out = head_items
        scores = jnp.dot(query, keys.T, preferred_element_type=jnp.float32) * softmax_scale
        scores = jnp.where(visible, scores, masked_value)
        peak = jnp.max(scores, axis=1, keepdims=True)
        weights = jnp.exp(scores - peak)
        probs = weights / jnp.sum(weights, axis=1, keepdims=True)
        grad_probs = jnp.dot(grad_out, latent_keys.T, preferred_element_type=jnp.float32)
        delta = jnp.sum(probs * grad_probs, axis=1, keepdims=True)
        grad_scores = (probs * (grad_probs - delta)).astype(jnp.bfloat16)
        probs_half = probs.astype(jnp.bfloat16)
        grad_query = (jnp.dot(grad_scores, keys, preferred_element_type=jnp.float32) * softmax_scale).astype(jnp.bfloat16)
        grad_key = jnp.dot(grad_scores.T, query, preferred_element_type=jnp.float32) * softmax_scale
        grad_value = jnp.dot(probs_half.T, grad_out, preferred_element_type=jnp.float32)
        grad_key = grad_key + jnp.pad(grad_value, ((0, 0), (0, ROPE)))
        return total + grad_key, grad_query

    start_total = jnp.zeros((SEQ, KDIM), jnp.float32)
    total, grad_heads = lax.scan(per_head, start_total, (jnp.swapaxes(queries, 0, 1), jnp.swapaxes(dout, 0, 1)))
    return jnp.swapaxes(grad_heads, 0, 1), total
```

```python
import functools

import jax
import jax.numpy as jnp
from jax import lax
from jax.experimental import pallas as pl
from jax.experimental.pallas import tpu as pltpu
from jax.sharding import PartitionSpec as P

softmax_scale = 0.1352
masked_value = -1e30
log2_e = 1.4426950408889634
tile = 256
nt_dims = (((1,), (1,)), ((), ()))


def attention_kernel(
    ctx_size, block_rows, heads, order_ref, q_ref, do_ref, qt_ref, dot_ref, *rest
):
    key_refs = rest[:ctx_size]
    dq_ref, keep_ref, send_ref = rest[ctx_size : ctx_size + 3]
    keys, scores, gprobs, peak, total, weighted, dq_acc, dkt, stage, in_sem, keep_sem, send_sem = rest[
        ctx_size + 3 :
    ]
    seq, width = keys.shape
    latent = do_ref.shape[1]
    rows = block_rows * heads
    me = lax.axis_index("ctx")

    def position(mask, sub):
        return order_ref[2 * jnp.bitwise_xor(me, mask) + sub]

    def sorted_rows(mask, sub):
        start = pl.multiple_of(position(mask, sub) * block_rows, 16)
        return pl.ds(start, block_rows)

    loads = []
    for mask in range(ctx_size):
        for sub in range(2):
            copy = pltpu.make_async_copy(
                key_refs[mask].at[pl.ds(sub * block_rows, block_rows), :],
                keys.at[sorted_rows(mask, sub), :],
                in_sem.at[2 * mask + sub],
            )
            copy.start()
            loads.append(copy)
    dkt[...] = jnp.zeros_like(dkt)
    for copy in loads:
        copy.wait()

    def key_tile(j):
        return pl.ds(pl.multiple_of(j * tile, tile), tile)

    for b in range(2):
        place = position(0, b)
        span = pl.ds(b * rows, rows)
        count = ((place + 1) * block_rows + tile - 1) // tile
        peak[...] = jnp.full_like(peak, masked_value)
        row_pos = place * block_rows + lax.broadcasted_iota(jnp.int32, (rows, tile), 0) // heads

        @pl.loop(0, count)
        def _(j):
            block = keys[key_tile(j), :]
            s = lax.dot_general(q_ref[span, :], block, nt_dims, preferred_element_type=jnp.float32)
            key_pos = j * tile + lax.broadcasted_iota(jnp.int32, (rows, tile), 1)
            s = jnp.where(key_pos <= row_pos, s, masked_value)
            scores[j] = s
            peak[...] = jnp.maximum(peak[...], jnp.maximum(s[:, :128], s[:, 128:]))
            gprobs[j] = lax.dot_general(
                do_ref[span, :], block[:, :latent], nt_dims, preferred_element_type=jnp.float32
            )

        peak[...] = jnp.broadcast_to(jnp.max(peak[...], axis=1, keepdims=True), peak.shape)
        total[...] = jnp.zeros_like(total)
        weighted[...] = jnp.zeros_like(weighted)

        @pl.loop(0, count)
        def _(j):
            m = peak[...]
            for half in range(2):
                cols = slice(half * 128, half * 128 + 128)
                p = jnp.exp2((scores[j, :, cols] - m) * (softmax_scale * log2_e))
                scores[j, :, cols] = p
                total[...] += p
                weighted[...] += p * gprobs[j, :, cols]

        inverse = 1.0 / jnp.sum(total[...], axis=1, keepdims=True)
        delta = jnp.sum(weighted[...], axis=1, keepdims=True) * inverse
        total[...] = jnp.broadcast_to(inverse, total.shape)
        weighted[...] = jnp.broadcast_to(delta, weighted.shape)
        dq_acc[...] = jnp.zeros_like(dq_acc)

        @pl.loop(0, count)
        def _(j):
            inv = jnp.concatenate([total[...]] * 2, axis=1)
            dlt = jnp.concatenate([weighted[...]] * 2, axis=1)
            p = scores[j] * inv
            ds = (p * (gprobs[j] - dlt)).astype(jnp.bfloat16)
            ph = p.astype(jnp.bfloat16)
            dq_acc[...] += jnp.dot(ds, keys[key_tile(j), :], preferred_element_type=jnp.float32)
            dkt[j] += (
                jnp.dot(qt_ref[:, span], ds, preferred_element_type=jnp.float32) * softmax_scale
            )
            dkt[j, :latent, :] += jnp.dot(
                dot_ref[:, span], ph, preferred_element_type=jnp.float32
            )

        dq_ref[span, :] = (dq_acc[...] * softmax_scale).astype(jnp.bfloat16)

    @pl.loop(0, seq // tile)
    def _(j):
        stage[key_tile(j), :] = dkt[j].T

    copies = []
    for mask in range(ctx_size):
        for sub in range(2):
            out = keep_ref if mask % 2 == 0 else send_ref
            sem = keep_sem if mask % 2 == 0 else send_sem
            copy = pltpu.make_async_copy(
                stage.at[sorted_rows(mask, sub), :],
                out.at[mask // 2, pl.ds(sub * block_rows, block_rows), :],
                sem.at[2 * (mask // 2) + sub],
            )
            copy.start()
            copies.append(copy)
    for copy in copies:
        copy.wait()


def attention(order, q, do, qt, dot, key_list, ctx_size, block_rows, heads):
    total_rows, width = q.shape
    latent = do.shape[1]
    rows = block_rows * heads
    seq = 2 * block_rows * ctx_size
    half = ctx_size // 2
    tiles = seq // tile
    vmem = pl.BlockSpec(memory_space=pltpu.VMEM)
    anywhere = pl.BlockSpec(memory_space=pl.ANY)
    return pl.pallas_call(
        functools.partial(attention_kernel, ctx_size, block_rows, heads),
        out_shape=(
            jax.ShapeDtypeStruct((total_rows, width), jnp.bfloat16),
            jax.ShapeDtypeStruct((half, 2 * block_rows, width), jnp.float32),
            jax.ShapeDtypeStruct((half, 2 * block_rows, width), jnp.float32),
        ),
        in_specs=[pl.BlockSpec(memory_space=pltpu.SMEM)] + [vmem] * 4 + [anywhere] * ctx_size,
        out_specs=(vmem, anywhere, anywhere),
        scratch_shapes=[
            pltpu.VMEM((seq, width), jnp.bfloat16),
            pltpu.VMEM((tiles, rows, tile), jnp.float32),
            pltpu.VMEM((tiles, rows, tile), jnp.float32),
            pltpu.VMEM((rows, 128), jnp.float32),
            pltpu.VMEM((rows, 128), jnp.float32),
            pltpu.VMEM((rows, 128), jnp.float32),
            pltpu.VMEM((rows, width), jnp.float32),
            pltpu.VMEM((tiles, width, tile), jnp.float32),
            pltpu.VMEM((seq, width), jnp.float32),
            pltpu.SemaphoreType.DMA((2 * ctx_size,)),
            pltpu.SemaphoreType.DMA((ctx_size,)),
            pltpu.SemaphoreType.DMA((ctx_size,)),
        ],
        compiler_params=pltpu.CompilerParams(vmem_limit_bytes=62 * 1024 * 1024),
        name="attention_backward",
    )(order, q, do, qt, dot, *key_list)


def per_device(block_order, queries, keys, dout):
    token_count, head_count, key_width = queries.shape
    latent_width = dout.shape[2]
    block_rows = token_count // 2
    ctx_size = lax.axis_size("ctx")
    head_size = lax.axis_size("head")

    def swap(x, axis, mask):
        size = lax.axis_size(axis)
        return lax.ppermute(x, axis, [(i, i ^ mask) for i in range(size)])

    query_rows = queries.reshape(token_count * head_count, key_width)
    grad_rows = dout.reshape(token_count * head_count, latent_width)
    same_core = [keys] + [swap(keys, "ctx", mask) for mask in range(2, ctx_size, 2)]
    key_list = []
    for block in same_core:
        key_list += [block, swap(block, "ctx", 1)]
    grad_query, keep, send = attention(
        block_order,
        query_rows,
        grad_rows,
        query_rows.T,
        grad_rows.T,
        key_list,
        ctx_size,
        block_rows,
        head_count,
    )
    grad_queries = grad_query.reshape(token_count, head_count, key_width)
    sums = keep + swap(send.astype(jnp.bfloat16), "ctx", 1).astype(jnp.float32)
    own = sums[0]
    parts = [
        swap(sums[mask // 2].astype(jnp.bfloat16), "ctx", mask) for mask in range(2, ctx_size, 2)
    ]
    for part in parts:
        own = own + part.astype(jnp.float32)
    own = lax.optimization_barrier(own.astype(jnp.bfloat16))
    level = [own] + [swap(own, "head", mask) for mask in range(1, head_size)]
    level = [x.astype(jnp.float32) for x in level]
    while len(level) > 1:
        level = [level[i] + level[i + 1] for i in range(0, len(level), 2)]
    return (grad_queries, level[0])


def solution(mesh):
    placed = (P(), P("ctx", "head", None), P("ctx", None), P("ctx", "head", None))
    return jax.shard_map(
        per_device,
        mesh=mesh,
        in_specs=placed,
        out_specs=(P("ctx", "head", None), P("ctx", None)),
        check_vma=False,
    )
```

```python
import functools

import jax
import jax.numpy as jnp
from jax import lax
from jax.experimental import pallas as pl
from jax.experimental.pallas import tpu as pltpu
from jax.sharding import PartitionSpec as P

softmax_scale = 0.1352
masked_value = -1e30
log2_e = 1.4426950408889634
tile = 256
lanes = 128
mebibyte = 1024 * 1024
nt_dims = (((1,), (1,)), ((), ()))


def padded(width):
    return -(-width // lanes) * lanes


def chip_axes(core, ctx_size):
    bits = ctx_size.bit_length() - 2
    return [2 << (t + core) % bits for t in range(bits)]


def chip_mask(label, core, ctx_size):
    return sum(axis for t, axis in enumerate(chip_axes(core, ctx_size)) if label >> t & 1)


def layout_kernel(rows, q_ref, do_ref, qp_ref, qt_ref, dot_ref):
    width = q_ref.shape[1]
    qp_ref[:, :width] = q_ref[...]
    qp_ref[:, width:] = jnp.zeros((qp_ref.shape[0], qp_ref.shape[1] - width), qp_ref.dtype)
    for b in range(2):
        span = slice(b * rows, b * rows + rows)
        qt_ref[b] = q_ref[span, :].T
        dot_ref[b] = do_ref[span, :].T


def attention_kernel(direct, ctx_size, block_rows, heads, latent, width, order_ref, *rest):
    q, do, qt, dot = rest[:4]
    key_refs = rest[4 : 4 + ctx_size]
    dq_ref, keep_ref, send_ref = rest[4 + ctx_size : 7 + ctx_size]
    (keys, stage, probs, gprobs, marks, peak, total, weighted, dq_acc, dkt, move_sem) = rest[7 + ctx_size :]
    seq = keys.shape[0]
    tiles = seq // tile
    rows = block_rows * heads
    me = lax.axis_index("ctx")

    def sorted_rows(mask, sub):
        position = order_ref[2 * jnp.bitwise_xor(me, mask) + sub]
        return pl.ds(pl.multiple_of(position * block_rows, 16), block_rows)

    def move(pairs):
        if direct:
            for source, target in pairs:
                target[...] = source[...]
            return
        copies = [
            pltpu.make_async_copy(source, target, move_sem.at[i])
            for i, (source, target) in enumerate(pairs)
        ]
        for copy in copies:
            copy.start()
        for copy in copies:
            copy.wait()

    blocks = [(mask, sub) for mask in range(ctx_size) for sub in range(2)]

    def sub_rows(sub):
        return pl.ds(sub * block_rows, block_rows)

    move(
        [
            (key_refs[mask].at[sub_rows(sub), :], keys.at[sorted_rows(mask, sub), :])
            for mask, sub in blocks
        ]
    )

    first = jnp.where(order_ref[2 * me] < order_ref[2 * me + 1], 0, 1)
    order = (first, 1 - first)
    places = [order_ref[2 * me + b] for b in order]
    counts = [((place + 1) * block_rows + tile - 1) // tile for place in places]

    @pl.loop(counts[0], counts[1])
    def _(j):
        dkt[j] = jnp.zeros(dkt.shape[1:], dkt.dtype)


    def key_rows(j, count):
        return pl.ds(pl.multiple_of(j * tile, tile), count * tile)

    def visits(count, visit):
        @pl.loop(0, count // 2)
        def _(i):
            visit(2 * i, 2)

        @pl.when(count % 2 == 1)
        def _():
            visit(count - 1, 1)

    def piece(h):
        return slice(h % 2 * lanes, h % 2 * lanes + lanes)

    for turn in range(2):
        b, place = order[turn], places[turn]
        span = pl.ds(pl.multiple_of(b * rows, rows), rows)
        peak[...] = jnp.full_like(peak, masked_value)
        total[...] = jnp.zeros_like(total)
        weighted[...] = jnp.zeros_like(weighted)

        def score_visit(j, n):
            block = keys[key_rows(j, n), :]
            s = lax.dot_general(q[span, :], block, nt_dims, preferred_element_type=jnp.float32)
            g = lax.dot_general(
                do[span, :], block[:, :latent], nt_dims, preferred_element_type=jnp.float32
            )
            row_pos = (
                place * block_rows
                - j * tile
                + lax.broadcasted_iota(jnp.int32, (rows, lanes), 0) // heads
            )
            col = lax.broadcasted_iota(jnp.int32, (rows, lanes), 1)
            parts = []
            for h in range(2 * n):
                u = s[:, h * lanes : h * lanes + lanes] * (softmax_scale * log2_e)
                parts.append(jnp.where(col + h * lanes <= row_pos, u, masked_value))
            old = peak[...]
            m = functools.reduce(jnp.maximum, parts, old)
            alpha = jnp.exp2(old - m)
            acc = total[...] * alpha
            wacc = weighted[...] * alpha
            for h in range(2 * n):
                p = jnp.exp2(parts[h] - m)
                gh = g[:, h * lanes : h * lanes + lanes]
                probs[j + h // 2, :, piece(h)] = p
                gprobs[j + h // 2, :, piece(h)] = gh
                acc += p
                wacc += p * gh
            peak[...] = m
            marks[j // 2] = m
            total[...] = acc
            weighted[...] = wacc

        visits(counts[turn], score_visit)

        top = jnp.max(peak[...], axis=1, keepdims=True)
        share = jnp.exp2(peak[...] - top)
        inverse = 1.0 / jnp.sum(total[...] * share, axis=1, keepdims=True)
        delta = jnp.sum(weighted[...] * share, axis=1, keepdims=True) * inverse
        peak[...] = jnp.broadcast_to(top, peak.shape)
        total[...] = jnp.broadcast_to(inverse, total.shape)
        weighted[...] = jnp.broadcast_to(delta, weighted.shape)
        dq_acc[...] = jnp.zeros_like(dq_acc)

        def grad_visit(j, n):
            factor = jnp.exp2(marks[j // 2] - peak[...]) * total[...]
            delta = weighted[...]
            halves, grads = [], []
            for h in range(2 * n):
                p = probs[j + h // 2, :, piece(h)] * factor
                g = gprobs[j + h // 2, :, piece(h)]
                halves.append(p.astype(jnp.bfloat16))
                grads.append((p * (g - delta)).astype(jnp.bfloat16))
            ds = jnp.concatenate(grads, axis=1)
            ph = jnp.concatenate(halves, axis=1)
            dq_acc[...] += jnp.dot(
                ds, keys[key_rows(j, n), :], preferred_element_type=jnp.float32
            )
            kt = jnp.dot(qt[b], ds, preferred_element_type=jnp.float32) * softmax_scale
            vt = jnp.dot(dot[b], ph, preferred_element_type=jnp.float32)
            for t in range(n):
                cols = slice(t * tile, t * tile + tile)
                low = kt[:latent, cols] + vt[:, cols]
                high = kt[latent:, cols]
                if turn == 0:
                    dkt[j + t, :latent, :] = low
                    dkt[j + t, latent:, :] = high
                else:
                    low = low + dkt[j + t, :latent, :]
                    high = high + dkt[j + t, latent:, :]
                    stage[key_rows(j + t, 1), :latent] = low.T.astype(jnp.bfloat16)
                    stage[key_rows(j + t, 1), latent:width] = high.T.astype(jnp.bfloat16)
                    stage[key_rows(j + t, 1), width:] = jnp.zeros(
                        (tile, stage.shape[1] - width), stage.dtype
                    )

        visits(counts[turn], grad_visit)
        dq_ref[span, :] = (dq_acc[:, :width] * softmax_scale).astype(jnp.bfloat16)

    @pl.loop(counts[1], tiles)
    def _(j):
        stage[key_rows(j, 1), :] = jnp.zeros((tile, stage.shape[1]), stage.dtype)

    core = me % 2
    leaving = []
    for label in range(ctx_size // 2):
        masks = [chip_mask(label, c, ctx_size) for c in range(2)]
        kept = jnp.where(core == 0, masks[0], masks[1])
        sent = jnp.where(core == 0, masks[1], masks[0]) + 1
        for mask, out in ((kept, keep_ref), (sent, send_ref)):
            for sub in range(2):
                source = stage.at[sorted_rows(mask, sub), :]
                leaving.append((source, out.at[label, sub_rows(sub), :]))
    move(leaving)


def row_layouts(q, do, rows):
    total_rows, width = q.shape
    latent = do.shape[1]
    vmem = pl.BlockSpec(memory_space=pltpu.VMEM)
    return pl.pallas_call(
        functools.partial(layout_kernel, rows),
        out_shape=(
            jax.ShapeDtypeStruct((total_rows, padded(width)), q.dtype),
            jax.ShapeDtypeStruct((2, width, rows), q.dtype),
            jax.ShapeDtypeStruct((2, latent, rows), q.dtype),
        ),
        in_specs=[vmem] * 2,
        out_specs=(vmem,) * 3,
        compiler_params=pltpu.CompilerParams(vmem_limit_bytes=24 * mebibyte),
        name="row_layouts",
    )(q, do)


def attention(order, qp, do, qt, dot, key_list, block_rows, heads, width):
    ctx_size = len(key_list)
    total_rows = qp.shape[0]
    latent = do.shape[1]
    rows = block_rows * heads
    seq = 2 * block_rows * ctx_size
    half = ctx_size // 2
    tiles = seq // tile
    vmem = pl.BlockSpec(memory_space=pltpu.VMEM)
    f32, bf16 = jnp.float32, jnp.bfloat16
    buffers = [
        ((seq, padded(width)), bf16),
        ((seq, padded(width)), bf16),
        ((tiles, rows, tile), f32),
        ((tiles, rows, tile), f32),
        (((tiles + 1) // 2, rows, lanes), f32),
        ((rows, lanes), f32),
        ((rows, lanes), f32),
        ((rows, lanes), f32),
        ((rows, padded(width)), f32),
        ((tiles, width, tile), f32),
    ]
    direct = seq <= 2048
    blocks = vmem if direct else pl.BlockSpec(memory_space=pl.ANY)
    limit = 42 if direct else 63
    return pl.pallas_call(
        functools.partial(attention_kernel, direct, ctx_size, block_rows, heads, latent, width),
        out_shape=(
            jax.ShapeDtypeStruct((total_rows, width), bf16),
            jax.ShapeDtypeStruct((half, 2 * block_rows, padded(width)), bf16),
            jax.ShapeDtypeStruct((half, 2 * block_rows, padded(width)), bf16),
        ),
        in_specs=[pl.BlockSpec(memory_space=pltpu.SMEM)] + [vmem] * 4 + [blocks] * ctx_size,
        out_specs=(vmem, blocks, blocks),
        scratch_shapes=[pltpu.VMEM(shape, dtype) for shape, dtype in buffers]
        + [pltpu.SemaphoreType.DMA((2 * ctx_size,))],
        compiler_params=pltpu.CompilerParams(vmem_limit_bytes=limit * mebibyte),
        name="attention_backward",
    )(order, qp, do, qt, dot, *key_list)


def swap(x, axis, mask):
    size = lax.axis_size(axis)
    return lax.ppermute(x, axis, [(i, i ^ mask) for i in range(size)])


def sum_over_heads(own):
    size = lax.axis_size("head")
    place = lax.axis_index("head")
    half = own.shape[0] // 2
    low = place % 2 == 0
    mine = jnp.where(low, own[:half], own[half:])
    other = jnp.where(low, own[half:], own[:half]).astype(jnp.bfloat16)
    part = mine + swap(other, "head", 1).astype(jnp.float32)
    mask = 2
    while mask < size:
        sent = lax.optimization_barrier(part.astype(jnp.bfloat16))
        part = sent.astype(jnp.float32) + swap(sent, "head", mask).astype(jnp.float32)
        mask *= 2
    done = lax.optimization_barrier(part.astype(jnp.bfloat16))
    back = swap(done, "head", 1)
    upper = jnp.where(low, done, back)
    lower = jnp.where(low, back, done)
    return jnp.concatenate([upper, lower]).astype(jnp.float32)


def per_device(block_order, queries, keys, dout):
    token_count, head_count, key_width = queries.shape
    latent_width = dout.shape[2]
    block_rows = token_count // 2
    ctx_size = lax.axis_size("ctx")

    query_rows = queries.reshape(token_count * head_count, key_width)
    grad_rows = dout.reshape(token_count * head_count, latent_width)
    qp, qt, dot = row_layouts(query_rows, grad_rows, block_rows * head_count)
    extra = padded(key_width) - key_width
    keys = jnp.pad(keys, ((0, 0), (0, extra)))
    same_core = [keys] + [swap(keys, "ctx", mask) for mask in range(2, ctx_size, 2)]
    same_core[-1], qp, qt, dot = lax.optimization_barrier((same_core[-1], qp, qt, dot))
    key_list = []
    for block in same_core:
        key_list += [block, swap(block, "ctx", 1)]
    grad_query, keep, send = attention(
        block_order, qp, grad_rows, qt, dot, key_list, block_rows, head_count, key_width
    )
    grad_queries = grad_query.reshape(token_count, head_count, key_width)
    sums = keep.astype(jnp.float32) + swap(send, "ctx", 1).astype(jnp.float32)
    while sums.shape[0] > 1:
        half = sums.shape[0] // 2
        step = half.bit_length() - 1
        pairs = [(i, i ^ chip_axes(i % 2, ctx_size)[step]) for i in range(ctx_size)]
        sums = sums[:half] + lax.ppermute(sums[half:].astype(jnp.bfloat16), "ctx", pairs).astype(
            jnp.float32
        )
    own = sums[0]
    return (grad_queries, sum_over_heads(own)[:, :key_width])


def solution(mesh):
    placed = (P(), P("ctx", "head", None), P("ctx", None), P("ctx", "head", None))
    return jax.shard_map(
        per_device,
        mesh=mesh,
        in_specs=placed,
        out_specs=(P("ctx", "head", None), P("ctx", None)),
        check_vma=False,
    )
```

```python
import functools

import jax
import jax.numpy as jnp
from jax import lax
from jax.experimental import pallas as pl
from jax.experimental.pallas import tpu as pltpu
from jax.sharding import PartitionSpec as P

softmax_scale = 0.1352
masked_value = -1e30
log2_e = 1.4426950408889634
tile = 256
lanes = 128
mebibyte = 1024 * 1024
nt_dims = (((1,), (1,)), ((), ()))


def padded(width):
    return -(-width // lanes) * lanes


def chip_axes(core, ctx_size):
    bits = ctx_size.bit_length() - 2
    return [2 << (t + core) % bits for t in range(bits)]


def chip_mask(label, core, ctx_size):
    return sum(axis for t, axis in enumerate(chip_axes(core, ctx_size)) if label >> t & 1)


def key_rows(j, count):
    return pl.ds(pl.multiple_of(j * tile, tile), count * tile)


def visits(count, visit, largest):
    @pl.loop(0, count // largest)
    def _(i):
        visit(i * largest, largest)

    size = largest // 2
    while size:

        @pl.when(count // size % 2 == 1)
        def _(size=size):
            visit(count // (2 * size) * (2 * size), size)

        size //= 2


def query_blocks(order_ref, me, block_rows):
    first = jnp.where(order_ref[2 * me] < order_ref[2 * me + 1], 0, 1)
    order = (first, 1 - first)
    places = [order_ref[2 * me + b] for b in order]
    counts = [((place + 1) * block_rows + tile - 1) // tile for place in places]
    return order, places, counts


def layout_kernel(rows, q_ref, do_ref, qp_ref, qt_ref, dot_ref):
    width = q_ref.shape[1]
    qp_ref[:, :width] = q_ref[...]
    qp_ref[:, width:] = jnp.zeros((qp_ref.shape[0], qp_ref.shape[1] - width), qp_ref.dtype)
    for b in range(2):
        span = slice(b * rows, b * rows + rows)
        qt_ref[b] = q_ref[span, :].T
        dot_ref[b] = do_ref[span, :].T


def attention_kernel(direct, ctx_size, block_rows, heads, latent, width, order_ref, *rest):
    q, do, qt, dot = rest[:4]
    key_refs = rest[4 : 4 + ctx_size]
    keep_ref, send_ref = rest[4 + ctx_size : 6 + ctx_size]
    if direct:
        keys, *ds_refs = rest[6 + ctx_size : 9 + ctx_size]
        stage, probs, gprobs, marks, peak, total, weighted, dkt = rest[9 + ctx_size :]
    else:
        dq_ref = rest[6 + ctx_size]
        stage, probs, gprobs, marks, peak, total, weighted, dkt, keys, dq_acc, move_sem = rest[
            7 + ctx_size :
        ]
    seq = keys.shape[0]
    tiles = seq // tile
    rows = block_rows * heads
    me = lax.axis_index("ctx")

    def sorted_rows(mask, sub):
        position = order_ref[2 * jnp.bitwise_xor(me, mask) + sub]
        return pl.ds(pl.multiple_of(position * block_rows, 16), block_rows)

    def move(pairs):
        if direct:
            for source, target in pairs:
                target[...] = source[...]
            return
        copies = [
            pltpu.make_async_copy(source, target, move_sem.at[i])
            for i, (source, target) in enumerate(pairs)
        ]
        for copy in copies:
            copy.start()
        for copy in copies:
            copy.wait()

    blocks = [(mask, sub) for mask in range(ctx_size) for sub in range(2)]

    def sub_rows(sub):
        return pl.ds(sub * block_rows, block_rows)

    if direct:
        keys[:, width:] = jnp.zeros((seq, keys.shape[1] - width), keys.dtype)
        for mask, sub in blocks:
            keys[sorted_rows(mask, sub), :width] = key_refs[mask][sub_rows(sub), :]
    else:
        move(
            [
                (key_refs[mask].at[sub_rows(sub), :], keys.at[sorted_rows(mask, sub), :])
                for mask, sub in blocks
            ]
        )

    order, places, counts = query_blocks(order_ref, me, block_rows)

    @pl.loop(counts[0], counts[1])
    def _(j):
        dkt[j] = jnp.zeros(dkt.shape[1:], dkt.dtype)


    def piece(h):
        return slice(h % 2 * lanes, h % 2 * lanes + lanes)

    for turn in range(2):
        b, place = order[turn], places[turn]
        span = pl.ds(pl.multiple_of(b * rows, rows), rows)
        peak[...] = jnp.full_like(peak, masked_value)
        total[...] = jnp.zeros_like(total)
        weighted[...] = jnp.zeros_like(weighted)

        def score_visit(j, n):
            block = keys[key_rows(j, n), :]
            s = lax.dot_general(q[span, :], block, nt_dims, preferred_element_type=jnp.float32)
            g = lax.dot_general(
                do[span, :], block[:, :latent], nt_dims, preferred_element_type=jnp.float32
            )
            row_pos = (
                place * block_rows
                - j * tile
                + lax.broadcasted_iota(jnp.int32, (rows, lanes), 0) // heads
            )
            col = lax.broadcasted_iota(jnp.int32, (rows, lanes), 1)
            parts = []
            for h in range(2 * n):
                u = s[:, h * lanes : h * lanes + lanes] * (softmax_scale * log2_e)
                parts.append(jnp.where(col + h * lanes <= row_pos, u, masked_value))
            old = peak[...]
            m = functools.reduce(jnp.maximum, parts, old)
            alpha = jnp.exp2(old - m)
            acc = total[...] * alpha
            wacc = weighted[...] * alpha
            for h in range(2 * n):
                p = jnp.exp2(parts[h] - m)
                gh = g[:, h * lanes : h * lanes + lanes]
                probs[j + h // 2, :, piece(h)] = p
                gprobs[j + h // 2, :, piece(h)] = gh
                acc += p
                wacc += p * gh
            peak[...] = m
            marks[j // 2] = m
            total[...] = acc
            weighted[...] = wacc

        visits(counts[turn], score_visit, 2)

        top = jnp.max(peak[...], axis=1, keepdims=True)
        share = jnp.exp2(peak[...] - top)
        inverse = 1.0 / jnp.sum(total[...] * share, axis=1, keepdims=True)
        delta = jnp.sum(weighted[...] * share, axis=1, keepdims=True) * inverse
        peak[...] = jnp.broadcast_to(top, peak.shape)
        total[...] = jnp.broadcast_to(inverse, total.shape)
        weighted[...] = jnp.broadcast_to(delta, weighted.shape)
        if not direct:
            dq_acc[...] = jnp.zeros_like(dq_acc)

        def grad_visit(j, n):
            factor = jnp.exp2(marks[j // 2] - peak[...]) * total[...]
            delta = weighted[...]
            halves, grads = [], []
            for h in range(2 * n):
                p = probs[j + h // 2, :, piece(h)] * factor
                g = gprobs[j + h // 2, :, piece(h)]
                halves.append(p.astype(jnp.bfloat16))
                grads.append((p * (g - delta)).astype(jnp.bfloat16))
            ds = jnp.concatenate(grads, axis=1)
            ph = jnp.concatenate(halves, axis=1)
            if direct:
                for t in range(n):
                    ds_refs[turn][j + t] = ds[:, t * tile : t * tile + tile]
            else:
                dq_acc[...] += jnp.dot(
                    ds, keys[key_rows(j, n), :], preferred_element_type=jnp.float32
                )
            kt = jnp.dot(qt[b], ds, preferred_element_type=jnp.float32) * softmax_scale
            vt = jnp.dot(dot[b], ph, preferred_element_type=jnp.float32)
            for t in range(n):
                cols = slice(t * tile, t * tile + tile)
                low = kt[:latent, cols] + vt[:, cols]
                high = kt[latent:, cols]
                if turn == 0:
                    dkt[j + t, :latent, :] = low
                    dkt[j + t, latent:, :] = high
                else:
                    low = low + dkt[j + t, :latent, :]
                    high = high + dkt[j + t, latent:, :]
                    stage[key_rows(j + t, 1), :latent] = low.T.astype(jnp.bfloat16)
                    stage[key_rows(j + t, 1), latent:width] = high.T.astype(jnp.bfloat16)
                    stage[key_rows(j + t, 1), width:] = jnp.zeros(
                        (tile, stage.shape[1] - width), stage.dtype
                    )

        visits(counts[turn], grad_visit, 2)
        if not direct:
            dq_ref[span, :] = (dq_acc[:, :width] * softmax_scale).astype(jnp.bfloat16)

    @pl.loop(counts[1], tiles)
    def _(j):
        stage[key_rows(j, 1), :] = jnp.zeros((tile, stage.shape[1]), stage.dtype)

    core = me % 2
    leaving = []
    for label in range(ctx_size // 2):
        masks = [chip_mask(label, c, ctx_size) for c in range(2)]
        kept = jnp.where(core == 0, masks[0], masks[1])
        sent = jnp.where(core == 0, masks[1], masks[0]) + 1
        for mask, out in ((kept, keep_ref), (sent, send_ref)):
            for sub in range(2):
                source = stage.at[sorted_rows(mask, sub), :]
                leaving.append((source, out.at[label, sub_rows(sub), :]))
    move(leaving)


def row_layouts(q, do, rows):
    total_rows, width = q.shape
    latent = do.shape[1]
    vmem = pl.BlockSpec(memory_space=pltpu.VMEM)
    return pl.pallas_call(
        functools.partial(layout_kernel, rows),
        out_shape=(
            jax.ShapeDtypeStruct((total_rows, padded(width)), q.dtype),
            jax.ShapeDtypeStruct((2, width, rows), q.dtype),
            jax.ShapeDtypeStruct((2, latent, rows), q.dtype),
        ),
        in_specs=[vmem] * 2,
        out_specs=(vmem,) * 3,
        compiler_params=pltpu.CompilerParams(vmem_limit_bytes=24 * mebibyte),
        name="row_layouts",
    )(q, do)


def query_kernel(block_rows, heads, order_ref, keys, ds0, ds1, dq_ref, acc):
    rows = block_rows * heads
    width = dq_ref.shape[1]
    order, places, counts = query_blocks(order_ref, lax.axis_index("ctx"), block_rows)
    for turn in range(2):
        acc[...] = jnp.zeros_like(acc)

        def visit(j, n, ds=(ds0, ds1)[turn]):
            left = jnp.concatenate([ds[j + t] for t in range(n)], axis=1)
            acc[...] += jnp.dot(left, keys[key_rows(j, n), :], preferred_element_type=jnp.float32)

        visits(counts[turn], visit, 4)
        span = pl.ds(pl.multiple_of(order[turn] * rows, rows), rows)
        dq_ref[span, :] = (acc[:, :width] * softmax_scale).astype(jnp.bfloat16)


def query_gradient(order, keys, ds0, ds1, block_rows, heads, width):
    total_rows = 2 * block_rows * heads
    vmem = pl.BlockSpec(memory_space=pltpu.VMEM)
    return pl.pallas_call(
        functools.partial(query_kernel, block_rows, heads),
        out_shape=jax.ShapeDtypeStruct((total_rows, width), jnp.bfloat16),
        in_specs=[pl.BlockSpec(memory_space=pltpu.SMEM)] + [vmem] * 3,
        out_specs=vmem,
        scratch_shapes=[pltpu.VMEM((block_rows * heads, keys.shape[1]), jnp.float32)],
        compiler_params=pltpu.CompilerParams(vmem_limit_bytes=24 * mebibyte),
        cost_estimate=pl.CostEstimate(
            flops=2 * total_rows * keys.shape[0] * width, bytes_accessed=0, transcendentals=0
        ),
        name="query_gradient",
    )(order, keys, ds0, ds1)


def attention(order, qp, do, qt, dot, key_list, block_rows, heads, width, direct):
    ctx_size = len(key_list)
    total_rows = qp.shape[0]
    latent = do.shape[1]
    rows = block_rows * heads
    seq = 2 * block_rows * ctx_size
    half = ctx_size // 2
    tiles = seq // tile
    vmem = pl.BlockSpec(memory_space=pltpu.VMEM)
    f32, bf16 = jnp.float32, jnp.bfloat16
    wide = padded(width)
    buffers = [
        ((seq, wide), bf16),
        ((tiles, rows, tile), f32),
        ((tiles, rows, tile), f32),
        (((tiles + 1) // 2, rows, lanes), f32),
        ((rows, lanes), f32),
        ((rows, lanes), f32),
        ((rows, lanes), f32),
        ((tiles, width, tile), f32),
    ]
    out_shape = [jax.ShapeDtypeStruct((half, 2 * block_rows, wide), bf16)] * 2
    if direct:
        out_shape += [
            jax.ShapeDtypeStruct((seq, wide), bf16),
            jax.ShapeDtypeStruct((tiles, rows, tile), bf16),
            jax.ShapeDtypeStruct((tiles, rows, tile), bf16),
        ]
        scratch = []
    else:
        out_shape += [jax.ShapeDtypeStruct((total_rows, width), bf16)]
        buffers += [((seq, wide), bf16), ((rows, wide), f32)]
        scratch = [pltpu.SemaphoreType.DMA((2 * ctx_size,))]
    blocks = vmem if direct else pl.BlockSpec(memory_space=pl.ANY)
    return pl.pallas_call(
        functools.partial(attention_kernel, direct, ctx_size, block_rows, heads, latent, width),
        out_shape=tuple(out_shape),
        in_specs=[pl.BlockSpec(memory_space=pltpu.SMEM)] + [vmem] * 4 + [blocks] * ctx_size,
        out_specs=(blocks, blocks) + (vmem,) * (len(out_shape) - 2),
        scratch_shapes=[pltpu.VMEM(shape, dtype) for shape, dtype in buffers] + scratch,
        compiler_params=pltpu.CompilerParams(
            vmem_limit_bytes=(32 if direct else 63) * mebibyte
        ),
        name="attention_backward",
    )(order, qp, do, qt, dot, *key_list)


def swap(x, axis, mask):
    size = lax.axis_size(axis)
    return lax.ppermute(x, axis, [(i, i ^ mask) for i in range(size)])


def sum_over_heads(own):
    size = lax.axis_size("head")
    place = lax.axis_index("head")
    half = own.shape[0] // 2
    low = place % 2 == 0
    mine = jnp.where(low, own[:half], own[half:])
    other = jnp.where(low, own[half:], own[:half]).astype(jnp.bfloat16)
    part = mine + swap(other, "head", 1).astype(jnp.float32)
    mask = 2
    while mask < size:
        sent = lax.optimization_barrier(part.astype(jnp.bfloat16))
        part = sent.astype(jnp.float32) + swap(sent, "head", mask).astype(jnp.float32)
        mask *= 2
    done = lax.optimization_barrier(part.astype(jnp.bfloat16))
    back = swap(done, "head", 1)
    upper = jnp.where(low, done, back)
    lower = jnp.where(low, back, done)
    return jnp.concatenate([upper, lower]).astype(jnp.float32)


def per_device(block_order, queries, keys, dout):
    token_count, head_count, key_width = queries.shape
    latent_width = dout.shape[2]
    block_rows = token_count // 2
    ctx_size = lax.axis_size("ctx")

    query_rows = queries.reshape(token_count * head_count, key_width)
    grad_rows = dout.reshape(token_count * head_count, latent_width)
    qp, qt, dot = row_layouts(query_rows, grad_rows, block_rows * head_count)
    direct = token_count * ctx_size <= 2048
    if not direct:
        keys = jnp.pad(keys, ((0, 0), (0, padded(key_width) - key_width)))
    same_core = [keys] + [swap(keys, "ctx", mask) for mask in range(2, ctx_size, 2)]
    same_core[-1], qp, qt, dot = lax.optimization_barrier((same_core[-1], qp, qt, dot))
    key_list = []
    for block in same_core:
        key_list += [block, swap(block, "ctx", 1)]
    keep, send, *found = attention(
        block_order, qp, grad_rows, qt, dot, key_list, block_rows, head_count, key_width, direct
    )
    sums = keep.astype(jnp.float32) + swap(send, "ctx", 1).astype(jnp.float32)
    if direct:
        sums, *found = lax.optimization_barrier((sums, *found))
        grad_query = query_gradient(block_order, *found, block_rows, head_count, key_width)
    else:
        grad_query = found[0]
    while sums.shape[0] > 1:
        half = sums.shape[0] // 2
        step = half.bit_length() - 1
        pairs = [(i, i ^ chip_axes(i % 2, ctx_size)[step]) for i in range(ctx_size)]
        arrived = lax.ppermute(sums[half:].astype(jnp.bfloat16), "ctx", pairs)
        if direct and sums.shape[0] == ctx_size // 2:
            arrived, grad_query = lax.optimization_barrier((arrived, grad_query))
        sums = sums[:half] + arrived.astype(jnp.float32)
    own = sums[0]
    grad_queries = grad_query.reshape(token_count, head_count, key_width)
    return (grad_queries, sum_over_heads(own)[:, :key_width])


def solution(mesh):
    placed = (P(), P("ctx", "head", None), P("ctx", None), P("ctx", "head", None))
    return jax.shard_map(
        per_device,
        mesh=mesh,
        in_specs=placed,
        out_specs=(P("ctx", "head", None), P("ctx", None)),
        check_vma=False,
    )
```

```python
import functools

import jax
import jax.numpy as jnp
from jax import lax
from jax.experimental import pallas as pl
from jax.experimental.pallas import tpu as pltpu
from jax.sharding import PartitionSpec as P

softmax_scale = 0.1352
masked_value = -1e30
log2_e = 1.4426950408889634
tile = 256
lanes = 128
mebibyte = 1024 * 1024
nt_dims = (((1,), (1,)), ((), ()))


def padded(width):
    return -(-width // lanes) * lanes


def chip_axes(core, ctx_size):
    bits = ctx_size.bit_length() - 2
    return [2 << (t + core) % bits for t in range(bits)]


def chip_mask(label, core, ctx_size):
    return sum(axis for t, axis in enumerate(chip_axes(core, ctx_size)) if label >> t & 1)


def key_rows(j, count):
    return pl.ds(pl.multiple_of(j * tile, tile), count * tile)


def visits(count, visit, largest):
    @pl.loop(0, count // largest)
    def _(i):
        visit(i * largest, largest)

    size = largest // 2
    while size:

        @pl.when(count // size % 2 == 1)
        def _(size=size):
            visit(count // (2 * size) * (2 * size), size)

        size //= 2


def query_blocks(order_ref, me, block_rows):
    first = jnp.where(order_ref[2 * me] < order_ref[2 * me + 1], 0, 1)
    order = (first, 1 - first)
    places = [order_ref[2 * me + b] for b in order]
    counts = [((place + 1) * block_rows + tile - 1) // tile for place in places]
    return order, places, counts


def layout_kernel(rows, q_ref, do_ref, qp_ref, qt_ref, dot_ref):
    width = q_ref.shape[1]
    qp_ref[:, :width] = q_ref[...]
    qp_ref[:, width:] = jnp.zeros((qp_ref.shape[0], qp_ref.shape[1] - width), qp_ref.dtype)
    for b in range(2):
        span = slice(b * rows, b * rows + rows)
        qt_ref[b] = q_ref[span, :].T
        dot_ref[b] = do_ref[span, :].T


def attention_kernel(direct, ctx_size, block_rows, heads, latent, width, order_ref, *rest):
    q, do, qt, dot = rest[:4]
    key_refs = rest[4 : 4 + ctx_size]
    outs = rest[4 + ctx_size : 8 + ctx_size]
    rest = rest[8 + ctx_size :]
    if direct:
        keys, *ds_refs = rest[:3]
        stage, probs, gprobs, marks, peak, total, weighted, dkt = rest[3:]
    else:
        dq_ref, stage, probs, gprobs, marks, peak, total, weighted, dkt, keys, dq_acc, move_sem = rest
    seq = keys.shape[0]
    tiles = seq // tile
    rows = block_rows * heads
    me = lax.axis_index("ctx")

    def sorted_rows(mask, sub):
        position = order_ref[2 * jnp.bitwise_xor(me, mask) + sub]
        return pl.ds(pl.multiple_of(position * block_rows, 16), block_rows)

    def move(pairs):
        if direct:
            for source, target in pairs:
                target[...] = source[...]
            return
        copies = [
            pltpu.make_async_copy(source, target, move_sem.at[i])
            for i, (source, target) in enumerate(pairs)
        ]
        for copy in copies:
            copy.start()
        for copy in copies:
            copy.wait()

    blocks = [(mask, sub) for mask in range(ctx_size) for sub in range(2)]

    def sub_rows(sub):
        return pl.ds(sub * block_rows, block_rows)

    if direct:
        keys[:, width:] = jnp.zeros((seq, keys.shape[1] - width), keys.dtype)
        for mask, sub in blocks:
            keys[sorted_rows(mask, sub), :width] = key_refs[mask][sub_rows(sub), :]
    else:
        move(
            [
                (key_refs[mask].at[sub_rows(sub), :], keys.at[sorted_rows(mask, sub), :])
                for mask, sub in blocks
            ]
        )

    order, places, counts = query_blocks(order_ref, me, block_rows)

    @pl.loop(counts[0], counts[1])
    def _(j):
        dkt[j] = jnp.zeros(dkt.shape[1:], dkt.dtype)


    def piece(h):
        return slice(h % 2 * lanes, h % 2 * lanes + lanes)

    for turn in range(2):
        b, place = order[turn], places[turn]
        span = pl.ds(pl.multiple_of(b * rows, rows), rows)
        peak[...] = jnp.full_like(peak, masked_value)
        total[...] = jnp.zeros_like(total)
        weighted[...] = jnp.zeros_like(weighted)

        def score_visit(j, n):
            block = keys[key_rows(j, n), :]
            s = lax.dot_general(q[span, :], block, nt_dims, preferred_element_type=jnp.float32)
            g = lax.dot_general(
                do[span, :], block[:, :latent], nt_dims, preferred_element_type=jnp.float32
            )
            row_pos = (
                place * block_rows
                - j * tile
                + lax.broadcasted_iota(jnp.int32, (rows, lanes), 0) // heads
            )
            col = lax.broadcasted_iota(jnp.int32, (rows, lanes), 1)
            parts = []
            for h in range(2 * n):
                u = s[:, h * lanes : h * lanes + lanes] * (softmax_scale * log2_e)
                parts.append(jnp.where(col + h * lanes <= row_pos, u, masked_value))
            old = peak[...]
            m = functools.reduce(jnp.maximum, parts, old)
            alpha = jnp.exp2(old - m)
            acc = total[...] * alpha
            wacc = weighted[...] * alpha
            for h in range(2 * n):
                p = jnp.exp2(parts[h] - m)
                gh = g[:, h * lanes : h * lanes + lanes]
                probs[j + h // 2, :, piece(h)] = p
                gprobs[j + h // 2, :, piece(h)] = gh
                acc += p
                wacc += p * gh
            peak[...] = m
            marks[j // 2] = m
            total[...] = acc
            weighted[...] = wacc

        visits(counts[turn], score_visit, 2)

        top = jnp.max(peak[...], axis=1, keepdims=True)
        share = jnp.exp2(peak[...] - top)
        inverse = 1.0 / jnp.sum(total[...] * share, axis=1, keepdims=True)
        delta = jnp.sum(weighted[...] * share, axis=1, keepdims=True) * inverse
        peak[...] = jnp.broadcast_to(top, peak.shape)
        total[...] = jnp.broadcast_to(inverse, total.shape)
        weighted[...] = jnp.broadcast_to(delta, weighted.shape)
        if not direct:
            dq_acc[...] = jnp.zeros_like(dq_acc)

        def grad_visit(j, n):
            factor = jnp.exp2(marks[j // 2] - peak[...]) * total[...]
            delta = weighted[...]
            halves, grads = [], []
            for h in range(2 * n):
                p = probs[j + h // 2, :, piece(h)] * factor
                g = gprobs[j + h // 2, :, piece(h)]
                halves.append(p.astype(jnp.bfloat16))
                grads.append((p * (g - delta)).astype(jnp.bfloat16))
            ds = jnp.concatenate(grads, axis=1)
            ph = jnp.concatenate(halves, axis=1)
            if direct:
                for t in range(n):
                    ds_refs[turn][j + t] = ds[:, t * tile : t * tile + tile]
            else:
                dq_acc[...] += jnp.dot(
                    ds, keys[key_rows(j, n), :], preferred_element_type=jnp.float32
                )
            kt = jnp.dot(qt[b], ds, preferred_element_type=jnp.float32) * softmax_scale
            vt = jnp.dot(dot[b], ph, preferred_element_type=jnp.float32)
            for t in range(n):
                cols = slice(t * tile, t * tile + tile)
                low = kt[:latent, cols] + vt[:, cols]
                high = kt[latent:, cols]
                if turn == 0:
                    dkt[j + t, :latent, :] = low
                    dkt[j + t, latent:, :] = high
                else:
                    low = low + dkt[j + t, :latent, :]
                    high = high + dkt[j + t, latent:, :]
                    stage[key_rows(j + t, 1), :latent] = low.T.astype(jnp.bfloat16)
                    stage[key_rows(j + t, 1), latent:width] = high.T.astype(jnp.bfloat16)
                    stage[key_rows(j + t, 1), width:] = jnp.zeros(
                        (tile, stage.shape[1] - width), stage.dtype
                    )

        visits(counts[turn], grad_visit, 2)
        if not direct:
            dq_ref[span, :] = (dq_acc[:, :width] * softmax_scale).astype(jnp.bfloat16)

    @pl.loop(counts[1], tiles)
    def _(j):
        stage[key_rows(j, 1), :] = jnp.zeros((tile, stage.shape[1]), stage.dtype)

    core = me % 2
    leaving = []
    for label in range(ctx_size // 2):
        masks = [chip_mask(label, c, ctx_size) for c in range(2)]
        kept = jnp.where(core == 0, masks[0], masks[1])
        sent = jnp.where(core == 0, masks[1], masks[0]) + 1
        upper, slot = divmod(label, ctx_size // 4)
        for mask, out in ((kept, outs[upper]), (sent, outs[2 + upper])):
            for sub in range(2):
                source = stage.at[sorted_rows(mask, sub), :]
                leaving.append((source, out.at[slot, sub_rows(sub), :]))
    move(leaving)


def row_layouts(q, do, rows):
    total_rows, width = q.shape
    latent = do.shape[1]
    vmem = pl.BlockSpec(memory_space=pltpu.VMEM)
    return pl.pallas_call(
        functools.partial(layout_kernel, rows),
        out_shape=(
            jax.ShapeDtypeStruct((total_rows, padded(width)), q.dtype),
            jax.ShapeDtypeStruct((2, width, rows), q.dtype),
            jax.ShapeDtypeStruct((2, latent, rows), q.dtype),
        ),
        in_specs=[vmem] * 2,
        out_specs=(vmem,) * 3,
        compiler_params=pltpu.CompilerParams(vmem_limit_bytes=24 * mebibyte),
        name="row_layouts",
    )(q, do)


def query_kernel(block_rows, heads, order_ref, keys, ds0, ds1, dq_ref, acc):
    rows = block_rows * heads
    width = dq_ref.shape[1]
    order, places, counts = query_blocks(order_ref, lax.axis_index("ctx"), block_rows)
    for turn in range(2):
        acc[...] = jnp.zeros_like(acc)

        def visit(j, n, ds=(ds0, ds1)[turn]):
            left = jnp.concatenate([ds[j + t] for t in range(n)], axis=1)
            acc[...] += jnp.dot(left, keys[key_rows(j, n), :], preferred_element_type=jnp.float32)

        visits(counts[turn], visit, 4)
        span = pl.ds(pl.multiple_of(order[turn] * rows, rows), rows)
        dq_ref[span, :] = (acc[:, :width] * softmax_scale).astype(jnp.bfloat16)


def query_gradient(order, keys, ds0, ds1, block_rows, heads, width):
    total_rows = 2 * block_rows * heads
    vmem = pl.BlockSpec(memory_space=pltpu.VMEM)
    return pl.pallas_call(
        functools.partial(query_kernel, block_rows, heads),
        out_shape=jax.ShapeDtypeStruct((total_rows, width), jnp.bfloat16),
        in_specs=[pl.BlockSpec(memory_space=pltpu.SMEM)] + [vmem] * 3,
        out_specs=vmem,
        scratch_shapes=[pltpu.VMEM((block_rows * heads, keys.shape[1]), jnp.float32)],
        compiler_params=pltpu.CompilerParams(vmem_limit_bytes=24 * mebibyte),
        cost_estimate=pl.CostEstimate(
            flops=2 * total_rows * keys.shape[0] * width, bytes_accessed=0, transcendentals=0
        ),
        name="query_gradient",
    )(order, keys, ds0, ds1)


def attention(order, qp, do, qt, dot, key_list, block_rows, heads, width, direct):
    ctx_size = len(key_list)
    total_rows = qp.shape[0]
    latent = do.shape[1]
    rows = block_rows * heads
    seq = 2 * block_rows * ctx_size
    tiles = seq // tile
    vmem = pl.BlockSpec(memory_space=pltpu.VMEM)
    f32, bf16 = jnp.float32, jnp.bfloat16
    wide = padded(width)
    buffers = [
        ((seq, wide), bf16),
        ((tiles, rows, tile), f32),
        ((tiles, rows, tile), f32),
        (((tiles + 1) // 2, rows, lanes), f32),
        ((rows, lanes), f32),
        ((rows, lanes), f32),
        ((rows, lanes), f32),
        ((tiles, width, tile), f32),
    ]
    out_shape = [jax.ShapeDtypeStruct((ctx_size // 4, 2 * block_rows, wide), bf16)] * 4
    if direct:
        out_shape += [
            jax.ShapeDtypeStruct((seq, wide), bf16),
            jax.ShapeDtypeStruct((tiles, rows, tile), bf16),
            jax.ShapeDtypeStruct((tiles, rows, tile), bf16),
        ]
        scratch = []
    else:
        out_shape += [jax.ShapeDtypeStruct((total_rows, width), bf16)]
        buffers += [((seq, wide), bf16), ((rows, wide), f32)]
        scratch = [pltpu.SemaphoreType.DMA((2 * ctx_size,))]
    blocks = vmem if direct else pl.BlockSpec(memory_space=pl.ANY)
    return pl.pallas_call(
        functools.partial(attention_kernel, direct, ctx_size, block_rows, heads, latent, width),
        out_shape=tuple(out_shape),
        in_specs=[pl.BlockSpec(memory_space=pltpu.SMEM)] + [vmem] * 4 + [blocks] * ctx_size,
        out_specs=(blocks,) * 4 + (vmem,) * (len(out_shape) - 4),
        scratch_shapes=[pltpu.VMEM(shape, dtype) for shape, dtype in buffers] + scratch,
        compiler_params=pltpu.CompilerParams(
            vmem_limit_bytes=(32 if direct else 63) * mebibyte
        ),
        name="attention_backward",
    )(order, qp, do, qt, dot, *key_list)


def swap(x, axis, mask):
    size = lax.axis_size(axis)
    return lax.ppermute(x, axis, [(i, i ^ mask) for i in range(size)])


def sum_over_heads(own):
    size = lax.axis_size("head")
    place = lax.axis_index("head")
    half = own.shape[0] // 2
    low = place % 2 == 0
    mine = jnp.where(low, own[:half], own[half:])
    other = jnp.where(low, own[half:], own[:half]).astype(jnp.bfloat16)
    part = mine + swap(other, "head", 1).astype(jnp.float32)
    mask = 2
    while mask < size:
        sent = lax.optimization_barrier(part.astype(jnp.bfloat16))
        part = sent.astype(jnp.float32) + swap(sent, "head", mask).astype(jnp.float32)
        mask *= 2
    done = lax.optimization_barrier(part.astype(jnp.bfloat16))
    back = swap(done, "head", 1)
    upper = jnp.where(low, done, back)
    lower = jnp.where(low, back, done)
    return jnp.concatenate([upper, lower]).astype(jnp.float32)


def per_device(block_order, queries, keys, dout):
    token_count, head_count, key_width = queries.shape
    latent_width = dout.shape[2]
    block_rows = token_count // 2
    ctx_size = lax.axis_size("ctx")

    query_rows = queries.reshape(token_count * head_count, key_width)
    grad_rows = dout.reshape(token_count * head_count, latent_width)
    qp, qt, dot = row_layouts(query_rows, grad_rows, block_rows * head_count)
    direct = token_count * ctx_size <= 2048
    if not direct:
        keys = jnp.pad(keys, ((0, 0), (0, padded(key_width) - key_width)))
    same_core = [keys] + [swap(keys, "ctx", mask) for mask in range(2, ctx_size, 2)]
    same_core[-1], qp, qt, dot = lax.optimization_barrier((same_core[-1], qp, qt, dot))
    key_list = []
    for block in same_core:
        key_list += [block, swap(block, "ctx", 1)]
    low, high, low_sent, high_sent, *found = attention(
        block_order, qp, grad_rows, qt, dot, key_list, block_rows, head_count, key_width, direct
    )

    def exchange(sums):
        step = sums.shape[0].bit_length() - 1
        pairs = [(i, i ^ chip_axes(i % 2, ctx_size)[step]) for i in range(ctx_size)]
        return lax.ppermute(sums.astype(jnp.bfloat16), "ctx", pairs).astype(jnp.float32)

    def both_cores(kept, sent):
        return kept.astype(jnp.float32) + swap(sent, "ctx", 1).astype(jnp.float32)

    high = both_cores(high, high_sent).astype(jnp.bfloat16)
    high, low, low_sent, *found = lax.optimization_barrier((high, low, low_sent, *found))
    arrived = exchange(high)
    sums = both_cores(low, low_sent)
    grad_query = found[0]
    if direct:
        grad_query = query_gradient(block_order, *found, block_rows, head_count, key_width)
        arrived, grad_query = lax.optimization_barrier((arrived, grad_query))
    grad_queries = grad_query.reshape(token_count, head_count, key_width)
    sums = sums + arrived
    while sums.shape[0] > 1:
        half = sums.shape[0] // 2
        sums = sums[:half] + exchange(sums[half:])
    own = sums[0]
    return (grad_queries, sum_over_heads(own)[:, :key_width])


def solution(mesh):
    placed = (P(), P("ctx", "head", None), P("ctx", None), P("ctx", "head", None))
    return jax.shard_map(
        per_device,
        mesh=mesh,
        in_specs=placed,
        out_specs=(P("ctx", "head", None), P("ctx", None)),
        check_vma=False,
    )
```

```python
import functools

import jax
import jax.numpy as jnp
from jax import lax
from jax.experimental import pallas as pl
from jax.experimental.pallas import tpu as pltpu
from jax.sharding import PartitionSpec as P

softmax_scale = 0.1352
masked_value = -1e30
log2_e = 1.4426950408889634
tile = 256
lanes = 128
mebibyte = 1024 * 1024
nt_dims = (((1,), (1,)), ((), ()))


def padded(width):
    return -(-width // lanes) * lanes


def chip_axes(core, ctx_size):
    bits = ctx_size.bit_length() - 2
    return [2 << (t + core) % bits for t in range(bits)]


def chip_mask(label, core, ctx_size):
    return sum(axis for t, axis in enumerate(chip_axes(core, ctx_size)) if label >> t & 1)


def key_rows(j, count):
    return pl.ds(pl.multiple_of(j * tile, tile), count * tile)


def visits(count, visit, largest):
    @pl.loop(0, count // largest)
    def _(i):
        visit(i * largest, largest)

    size = largest // 2
    while size:

        @pl.when(count // size % 2 == 1)
        def _(size=size):
            visit(count // (2 * size) * (2 * size), size)

        size //= 2


def query_blocks(order_ref, me, block_rows):
    first = jnp.where(order_ref[2 * me] < order_ref[2 * me + 1], 0, 1)
    order = (first, 1 - first)
    places = [order_ref[2 * me + b] for b in order]
    counts = [((place + 1) * block_rows + tile - 1) // tile for place in places]
    return order, places, counts


def layout_kernel(reorder, block_rows, order_ref, q_ref, do_ref, qp_ref, qt_ref, dot_ref):
    total_rows, width = q_ref.shape
    latent = do_ref.shape[1]
    rows = total_rows // 2
    order = range(2)
    if reorder:
        order, _, _ = query_blocks(order_ref, lax.axis_index("ctx"), block_rows)
        whole, rest = divmod(width, tile)
        for i in range(latent // tile):
            qp_ref[i] = do_ref[:, i * tile : i * tile + tile]
        for i in range(whole):
            qp_ref[latent // tile + i] = q_ref[:, i * tile : i * tile + tile]
        last = latent // tile + whole
        qp_ref[last, :, :rest] = q_ref[:, whole * tile :]
        qp_ref[last, :, rest:] = jnp.zeros((total_rows, tile - rest), qp_ref.dtype)
    else:
        qp_ref[:, :width] = q_ref[...]
        qp_ref[:, width:] = jnp.zeros((total_rows, qp_ref.shape[1] - width), qp_ref.dtype)
    for turn, b in enumerate(order):
        span = pl.ds(pl.multiple_of(b * rows, lanes), rows)
        qt_ref[:, turn * rows : turn * rows + rows] = q_ref[span, :].T
        dot_ref[:, turn * rows : turn * rows + rows] = do_ref[span, :].T


def sorted_block(order_ref, me, mask, sub, block_rows):
    position = order_ref[2 * jnp.bitwise_xor(me, mask) + sub]
    return pl.ds(pl.multiple_of(position * block_rows, 16), block_rows)


def sort_keys(order_ref, me, key_refs, keys, block_rows):
    width = key_refs[0].shape[1]
    keys[:, width:] = jnp.zeros((keys.shape[0], keys.shape[1] - width), keys.dtype)
    for mask, ref in enumerate(key_refs):
        for sub in range(2):
            keys[sorted_block(order_ref, me, mask, sub, block_rows), :width] = ref[
                sub * block_rows : sub * block_rows + block_rows, :
            ]


def leaving_blocks(me, ctx_size, outs):
    core = me % 2
    targets = []
    for label in range(ctx_size // 2):
        masks = [chip_mask(label, c, ctx_size) for c in range(2)]
        kept = jnp.where(core == 0, masks[0], masks[1])
        sent = jnp.where(core == 0, masks[1], masks[0]) + 1
        upper, slot = divmod(label, ctx_size // 4)
        for mask, out in ((kept, outs[upper]), (sent, outs[2 + upper])):
            targets += [(mask, sub, out, slot) for sub in range(2)]
    return targets


def short_kernel(ctx_size, block_rows, heads, latent, width, order_ref, work, qt, dot, *rest):
    key_refs, outs, rest = rest[:ctx_size], rest[ctx_size : ctx_size + 4], rest[ctx_size + 4 :]
    ds_ref, keys, scores, gprobs, peak, total, weighted = rest
    stage = keys
    seq = keys.shape[0]
    rows = block_rows * heads
    me = lax.axis_index("ctx")

    sort_keys(order_ref, me, key_refs, keys, block_rows)

    order, places, counts = query_blocks(order_ref, me, block_rows)
    spans = [pl.ds(pl.multiple_of(b * rows, lanes), rows) for b in order]

    def piece(h):
        return slice(h % 2 * lanes, h % 2 * lanes + lanes)

    for turn in range(2):
        span, place = spans[turn], places[turn]
        peak[turn] = jnp.full(peak.shape[1:], masked_value, jnp.float32)
        total[turn] = jnp.zeros(total.shape[1:], jnp.float32)
        weighted[turn] = jnp.zeros(weighted.shape[1:], jnp.float32)

        def score_visit(j, n):
            block = keys[key_rows(j, n), :]
            whole = range(latent // tile, (latent + width) // tile)
            q = jnp.concatenate(
                [work[i, span, :] for i in whole] + [work[whole.stop, span, :lanes]], axis=1
            )
            do = jnp.concatenate([work[i, span, :] for i in range(latent // tile)], axis=1)
            s = lax.dot_general(q, block, nt_dims, preferred_element_type=jnp.float32)
            g = lax.dot_general(
                do, block[:, :latent], nt_dims, preferred_element_type=jnp.float32
            )
            row_pos = (
                place * block_rows
                - j * tile
                + lax.broadcasted_iota(jnp.int32, (rows, lanes), 0) // heads
            )
            col = lax.broadcasted_iota(jnp.int32, (rows, lanes), 1)
            parts = []
            for h in range(2 * n):
                u = s[:, h * lanes : h * lanes + lanes] * (softmax_scale * log2_e)
                parts.append(jnp.where(col + h * lanes <= row_pos, u, masked_value))
            old = peak[turn]
            m = functools.reduce(jnp.maximum, parts, old)
            alpha = jnp.exp2(old - m)
            acc = total[turn] * alpha
            wacc = weighted[turn] * alpha
            for h in range(2 * n):
                p = jnp.exp2(parts[h] - m)
                gh = g[:, h * lanes : h * lanes + lanes]
                scores[turn, j + h // 2, :, piece(h)] = parts[h]
                gprobs[turn, j + h // 2, :, piece(h)] = gh
                acc += p
                wacc += p * gh
            peak[turn] = m
            total[turn] = acc
            weighted[turn] = wacc

        visits(counts[turn], score_visit, 2)

        top = jnp.max(peak[turn], axis=1, keepdims=True)
        share = jnp.exp2(peak[turn] - top)
        inverse = 1.0 / jnp.sum(total[turn] * share, axis=1, keepdims=True)
        delta = jnp.sum(weighted[turn] * share, axis=1, keepdims=True) * inverse
        peak[turn] = jnp.broadcast_to(top, peak.shape[1:])
        total[turn] = jnp.broadcast_to(inverse, total.shape[1:])
        weighted[turn] = jnp.broadcast_to(delta, weighted.shape[1:])

    def row_gradients(turn, j, n):
        grads, probs = [], []
        for h in range(2 * n):
            p = jnp.exp2(scores[turn, j + h // 2, :, piece(h)] - peak[turn]) * total[turn]
            g = gprobs[turn, j + h // 2, :, piece(h)]
            probs.append(p.astype(jnp.bfloat16))
            grads.append((p * (g - weighted[turn])).astype(jnp.bfloat16))
        ds, ph = jnp.concatenate(grads, axis=1), jnp.concatenate(probs, axis=1)
        for t in range(n):
            ds_ref[j + t, turn * rows : turn * rows + rows, :] = ds[:, t * tile : t * tile + tile]
        return ds, ph

    def key_sums(j, n, left, right, ds, ph):
        kt = jnp.dot(left, ds, preferred_element_type=jnp.float32) * softmax_scale
        vt = jnp.dot(right, ph, preferred_element_type=jnp.float32)
        for t in range(n):
            cols = slice(t * tile, t * tile + tile)
            out = key_rows(j + t, 1)
            stage[out, :latent] = (kt[:latent, cols] + vt[:, cols]).T.astype(jnp.bfloat16)
            stage[out, latent:width] = kt[latent:, cols].T.astype(jnp.bfloat16)
            stage[out, width:] = jnp.zeros((tile, stage.shape[1] - width), stage.dtype)

    def both_visit(j, n):
        pairs = zip(row_gradients(0, j, n), row_gradients(1, j, n))
        key_sums(j, n, qt[...], dot[...], *(jnp.concatenate(pair, axis=0) for pair in pairs))

    def later_visit(j, n):
        j = counts[0] + j
        key_sums(j, n, qt[:, rows:], dot[:, rows:], *row_gradients(1, j, n))

    visits(counts[0], both_visit, 2)
    visits(counts[1] - counts[0], later_visit, 2)

    @pl.loop(counts[1], seq // tile)
    def _(j):
        stage[key_rows(j, 1), :] = jnp.zeros((tile, stage.shape[1]), stage.dtype)

    for mask, sub, out, slot in leaving_blocks(me, ctx_size, outs):
        out[slot, sub * block_rows : sub * block_rows + block_rows, :] = stage[
            sorted_block(order_ref, me, mask, sub, block_rows), :
        ]


def long_kernel(ctx_size, block_rows, heads, latent, width, order_ref, *rest):
    q, do, qt, dot = rest[:4]
    key_refs = rest[4 : 4 + ctx_size]
    outs = rest[4 + ctx_size : 8 + ctx_size]
    rest = rest[8 + ctx_size :]
    dq_ref, stage, probs, gprobs, marks, peak, total, weighted, dkt, keys, dq_acc, move_sem = rest
    seq = keys.shape[0]
    tiles = seq // tile
    rows = block_rows * heads
    me = lax.axis_index("ctx")

    def sorted_rows(mask, sub):
        return sorted_block(order_ref, me, mask, sub, block_rows)

    def move(pairs):
        copies = [
            pltpu.make_async_copy(source, target, move_sem.at[i])
            for i, (source, target) in enumerate(pairs)
        ]
        for copy in copies:
            copy.start()
        for copy in copies:
            copy.wait()

    blocks = [(mask, sub) for mask in range(ctx_size) for sub in range(2)]

    def sub_rows(sub):
        return pl.ds(sub * block_rows, block_rows)

    move(
        [
            (key_refs[mask].at[sub_rows(sub), :], keys.at[sorted_rows(mask, sub), :])
            for mask, sub in blocks
        ]
    )

    order, places, counts = query_blocks(order_ref, me, block_rows)

    @pl.loop(counts[0], counts[1])
    def _(j):
        dkt[j] = jnp.zeros(dkt.shape[1:], dkt.dtype)


    def piece(h):
        return slice(h % 2 * lanes, h % 2 * lanes + lanes)

    for turn in range(2):
        b, place = order[turn], places[turn]
        span = pl.ds(pl.multiple_of(b * rows, lanes), rows)
        peak[...] = jnp.full_like(peak, masked_value)
        total[...] = jnp.zeros_like(total)
        weighted[...] = jnp.zeros_like(weighted)

        def score_visit(j, n):
            block = keys[key_rows(j, n), :]
            s = lax.dot_general(q[span, :], block, nt_dims, preferred_element_type=jnp.float32)
            g = lax.dot_general(
                do[span, :], block[:, :latent], nt_dims, preferred_element_type=jnp.float32
            )
            row_pos = (
                place * block_rows
                - j * tile
                + lax.broadcasted_iota(jnp.int32, (rows, lanes), 0) // heads
            )
            col = lax.broadcasted_iota(jnp.int32, (rows, lanes), 1)
            parts = []
            for h in range(2 * n):
                u = s[:, h * lanes : h * lanes + lanes] * (softmax_scale * log2_e)
                parts.append(jnp.where(col + h * lanes <= row_pos, u, masked_value))
            old = peak[...]
            m = functools.reduce(jnp.maximum, parts, old)
            alpha = jnp.exp2(old - m)
            acc = total[...] * alpha
            wacc = weighted[...] * alpha
            for h in range(2 * n):
                p = jnp.exp2(parts[h] - m)
                gh = g[:, h * lanes : h * lanes + lanes]
                probs[j + h // 2, :, piece(h)] = p
                gprobs[j + h // 2, :, piece(h)] = gh
                acc += p
                wacc += p * gh
            peak[...] = m
            marks[j // 2] = m
            total[...] = acc
            weighted[...] = wacc

        visits(counts[turn], score_visit, 2)

        top = jnp.max(peak[...], axis=1, keepdims=True)
        share = jnp.exp2(peak[...] - top)
        inverse = 1.0 / jnp.sum(total[...] * share, axis=1, keepdims=True)
        delta = jnp.sum(weighted[...] * share, axis=1, keepdims=True) * inverse
        peak[...] = jnp.broadcast_to(top, peak.shape)
        total[...] = jnp.broadcast_to(inverse, total.shape)
        weighted[...] = jnp.broadcast_to(delta, weighted.shape)
        dq_acc[...] = jnp.zeros_like(dq_acc)

        def grad_visit(j, n):
            factor = jnp.exp2(marks[j // 2] - peak[...]) * total[...]
            delta = weighted[...]
            halves, grads = [], []
            for h in range(2 * n):
                p = probs[j + h // 2, :, piece(h)] * factor
                g = gprobs[j + h // 2, :, piece(h)]
                halves.append(p.astype(jnp.bfloat16))
                grads.append((p * (g - delta)).astype(jnp.bfloat16))
            ds = jnp.concatenate(grads, axis=1)
            ph = jnp.concatenate(halves, axis=1)
            dq_acc[...] += jnp.dot(ds, keys[key_rows(j, n), :], preferred_element_type=jnp.float32)
            kt = jnp.dot(qt[:, span], ds, preferred_element_type=jnp.float32) * softmax_scale
            vt = jnp.dot(dot[:, span], ph, preferred_element_type=jnp.float32)
            for t in range(n):
                cols = slice(t * tile, t * tile + tile)
                low = kt[:latent, cols] + vt[:, cols]
                high = kt[latent:, cols]
                if turn == 0:
                    dkt[j + t, :latent, :] = low
                    dkt[j + t, latent:, :] = high
                else:
                    low = low + dkt[j + t, :latent, :]
                    high = high + dkt[j + t, latent:, :]
                    stage[key_rows(j + t, 1), :latent] = low.T.astype(jnp.bfloat16)
                    stage[key_rows(j + t, 1), latent:width] = high.T.astype(jnp.bfloat16)
                    stage[key_rows(j + t, 1), width:] = jnp.zeros(
                        (tile, stage.shape[1] - width), stage.dtype
                    )

        visits(counts[turn], grad_visit, 2)
        dq_ref[span, :] = (dq_acc[:, :width] * softmax_scale).astype(jnp.bfloat16)

    @pl.loop(counts[1], tiles)
    def _(j):
        stage[key_rows(j, 1), :] = jnp.zeros((tile, stage.shape[1]), stage.dtype)

    targets = leaving_blocks(me, ctx_size, outs)
    move([(stage.at[sorted_rows(mask, sub), :], out.at[slot, sub_rows(sub), :]) for mask, sub, out, slot in targets])


def row_layouts(order, q, do, block_rows, reorder, tiles):
    total_rows, width = q.shape
    latent = do.shape[1]
    vmem = pl.BlockSpec(memory_space=pltpu.VMEM)
    return pl.pallas_call(
        functools.partial(layout_kernel, reorder, block_rows),
        out_shape=(
            jax.ShapeDtypeStruct(
                (tiles, total_rows, tile) if reorder else (total_rows, padded(width)), q.dtype
            ),
            jax.ShapeDtypeStruct((width, total_rows), q.dtype),
            jax.ShapeDtypeStruct((latent, total_rows), q.dtype),
        ),
        in_specs=[pl.BlockSpec(memory_space=pltpu.SMEM)] + [vmem] * 2,
        out_specs=(vmem,) * 3,
        compiler_params=pltpu.CompilerParams(vmem_limit_bytes=24 * mebibyte),
        name="row_layouts",
    )(order, q, do)


def query_kernel(block_rows, order_ref, ds, *rest):
    *key_refs, dq_ref, keys, acc = rest
    me = lax.axis_index("ctx")
    sort_keys(order_ref, me, key_refs, keys, block_rows)
    order, _, counts = query_blocks(order_ref, me, block_rows)
    rows, width = dq_ref.shape[0] // 2, dq_ref.shape[1]
    acc[...] = jnp.zeros_like(acc)

    def add(j, n, span):
        left = jnp.concatenate([ds[j + t, span, :] for t in range(n)], axis=1)
        acc[span, :] += jnp.dot(left, keys[key_rows(j, n), :], preferred_element_type=jnp.float32)

    visits(counts[0], lambda j, n: add(j, n, slice(None)), 4)
    visits(counts[1] - counts[0], lambda j, n: add(counts[0] + j, n, slice(rows, 2 * rows)), 2)
    for turn in range(2):
        span = pl.ds(pl.multiple_of(order[turn] * rows, lanes), rows)
        dq_ref[span, :] = (
            acc[turn * rows : turn * rows + rows, :width] * softmax_scale
        ).astype(jnp.bfloat16)


def query_gradient(order, ds, key_list, block_rows):
    total_rows = ds.shape[1]
    block, width = key_list[0].shape
    keys = (len(key_list) * block, padded(width))
    vmem = pl.BlockSpec(memory_space=pltpu.VMEM)
    return pl.pallas_call(
        functools.partial(query_kernel, block_rows),
        out_shape=jax.ShapeDtypeStruct((total_rows, width), jnp.bfloat16),
        in_specs=[pl.BlockSpec(memory_space=pltpu.SMEM)] + [vmem] * (1 + len(key_list)),
        out_specs=vmem,
        scratch_shapes=[
            pltpu.VMEM(keys, jnp.bfloat16),
            pltpu.VMEM((total_rows, keys[1]), jnp.float32),
        ],
        compiler_params=pltpu.CompilerParams(vmem_limit_bytes=32 * mebibyte),
        cost_estimate=pl.CostEstimate(
            flops=2 * total_rows * keys[0] * width, bytes_accessed=0, transcendentals=0
        ),
        name="query_gradient",
    )(order, ds, *key_list)


def attention(order, row_arrays, key_list, block_rows, heads, width, direct):
    ctx_size = len(key_list)
    latent, total_rows = row_arrays[-1].shape
    rows = block_rows * heads
    seq = 2 * block_rows * ctx_size
    tiles = seq // tile
    vmem = pl.BlockSpec(memory_space=pltpu.VMEM)
    f32, bf16 = jnp.float32, jnp.bfloat16
    wide = padded(width)
    out_shape = [jax.ShapeDtypeStruct((ctx_size // 4, 2 * block_rows, wide), bf16)] * 4
    buffers = [((seq, wide), bf16)]
    scratch = []
    if direct:
        out_shape += [jax.ShapeDtypeStruct((tiles, total_rows, tile), bf16)]
        buffers += [((2, tiles, rows, tile), f32)] * 2
        buffers += [((2, rows, lanes), f32)] * 3
    else:
        out_shape += [jax.ShapeDtypeStruct((total_rows, width), bf16)]
        buffers += [((tiles, rows, tile), f32)] * 2 + [(((tiles + 1) // 2, rows, lanes), f32)]
        buffers += [((rows, lanes), f32)] * 3 + [((tiles, width, tile), f32)]
        buffers += [((seq, wide), bf16), ((rows, wide), f32)]
        scratch = [pltpu.SemaphoreType.DMA((2 * ctx_size,))]
    blocks = vmem if direct else pl.BlockSpec(memory_space=pl.ANY)
    return pl.pallas_call(
        functools.partial(
            short_kernel if direct else long_kernel, ctx_size, block_rows, heads, latent, width
        ),
        out_shape=tuple(out_shape),
        in_specs=[pl.BlockSpec(memory_space=pltpu.SMEM)]
        + [vmem] * len(row_arrays)
        + [blocks] * ctx_size,
        out_specs=(blocks,) * 4 + (vmem,) * (len(out_shape) - 4),
        input_output_aliases={1: 4} if direct else {},
        scratch_shapes=[pltpu.VMEM(shape, dtype) for shape, dtype in buffers] + scratch,
        compiler_params=pltpu.CompilerParams(
            vmem_limit_bytes=(37 if direct else 63) * mebibyte
        ),
        name="attention_backward",
    )(order, *row_arrays, *key_list)


def swap(x, axis, mask):
    size = lax.axis_size(axis)
    return lax.ppermute(x, axis, [(i, i ^ mask) for i in range(size)])


def sum_over_heads(own):
    size = lax.axis_size("head")
    place = lax.axis_index("head")
    half = own.shape[0] // 2
    low = place % 2 == 0
    mine = jnp.where(low, own[:half], own[half:])
    other = jnp.where(low, own[half:], own[:half]).astype(jnp.bfloat16)
    part = mine + swap(other, "head", 1).astype(jnp.float32)
    mask = 2
    while mask < size:
        sent = lax.optimization_barrier(part.astype(jnp.bfloat16))
        part = sent.astype(jnp.float32) + swap(sent, "head", mask).astype(jnp.float32)
        mask *= 2
    done = lax.optimization_barrier(part.astype(jnp.bfloat16))
    back = swap(done, "head", 1)
    upper = jnp.where(low, done, back)
    lower = jnp.where(low, back, done)
    return jnp.concatenate([upper, lower]).astype(jnp.float32)


def per_device(block_order, queries, keys, dout):
    token_count, head_count, key_width = queries.shape
    latent_width = dout.shape[2]
    block_rows = token_count // 2
    ctx_size = lax.axis_size("ctx")

    query_rows = queries.reshape(token_count * head_count, key_width)
    grad_rows = dout.reshape(token_count * head_count, latent_width)
    direct = token_count * ctx_size <= 2048
    tiles = token_count * ctx_size // tile
    qp, qt, dot = row_layouts(block_order, query_rows, grad_rows, block_rows, direct, tiles)
    if not direct:
        keys = jnp.pad(keys, ((0, 0), (0, padded(key_width) - key_width)))
    same_core = [keys] + [swap(keys, "ctx", mask) for mask in range(2, ctx_size, 2)]
    same_core[-1], qp, qt, dot = lax.optimization_barrier((same_core[-1], qp, qt, dot))
    key_list = []
    for block in same_core:
        key_list += [block, swap(block, "ctx", 1)]
    low, high, low_sent, high_sent, *found = attention(
        block_order,
        (qp, qt, dot) if direct else (qp, grad_rows, qt, dot),
        key_list,
        block_rows,
        head_count,
        key_width,
        direct,
    )

    def exchange(sums):
        step = sums.shape[0].bit_length() - 1
        pairs = [(i, i ^ chip_axes(i % 2, ctx_size)[step]) for i in range(ctx_size)]
        return lax.ppermute(sums.astype(jnp.bfloat16), "ctx", pairs).astype(jnp.float32)

    def both_cores(kept, sent):
        return kept.astype(jnp.float32) + swap(sent, "ctx", 1).astype(jnp.float32)

    high = both_cores(high, high_sent).astype(jnp.bfloat16)
    high, low, low_sent, *found = lax.optimization_barrier((high, low, low_sent, *found))
    arrived = exchange(high)
    sums = both_cores(low, low_sent)
    grad_query = found[0]
    if direct:
        grad_query = query_gradient(block_order, *found, key_list, block_rows)
        arrived, grad_query = lax.optimization_barrier((arrived, grad_query))
    grad_queries = grad_query.reshape(token_count, head_count, key_width)
    sums = sums + arrived
    while sums.shape[0] > 1:
        half = sums.shape[0] // 2
        sums = sums[:half] + exchange(sums[half:])
    own = sums[0]
    return (grad_queries, sum_over_heads(own)[:, :key_width])


def solution(mesh):
    placed = (P(), P("ctx", "head", None), P("ctx", None), P("ctx", "head", None))
    return jax.shard_map(
        per_device,
        mesh=mesh,
        in_specs=placed,
        out_specs=(P("ctx", "head", None), P("ctx", None)),
        check_vma=False,
    )
```
